256 devices in a mesh: section: 8 (over z), uly: 32 (over x, y, core).
Axes of the slice: x: 4, y: 4, z: 8, core: 2. Of those that a mesh axis runs over, the one named last changes fastest.
Arguments:
- query: bfloat16 [8, 1536, 4096], P('section', 'uly')
- fresh_keys: bfloat16 [8, 1536, 4096], P('section', 'uly'), may hold values from -6 to 6
- fresh_values: bfloat16 [8, 1536, 4096], P('section', 'uly'), may hold values from -6 to 6
- stale_keys: bfloat16 [8, 12288, 4096], P('section', None, 'uly')
- stale_values: bfloat16 [8, 12288, 4096], P('section', None, 'uly'), may hold values from -6 to 6
- next_gain: float32 [8, 4096], P('section'), may hold values from 0.1 to 1.9
- patch_index: int32 [8], P('section'), may hold values from 0 to 7, as said below
Outputs:
- handoff: bfloat16 [8, 1536, 4096], P('section', 'uly')
The draws below stay inside these ranges and needn't reach their ends.
Inputs may be any that keep to these rules, and one draw needn't show every extreme that they name: patch_index[s] = (t - s) mod 8 for one tick t of 0 to 6.
All inputs are finite; a program needn't handle non-finite values.
Results may differ from the reference program's by a relative error of at most 0.01.
Values may be sent and summed in bfloat16 or wider, within the bound.
A program may use at most 64 MiB of HBM per device.

```python
import jax
import jax.numpy as jnp
from jax import lax

HD = 128
HEADS = 32
D = 4096
PATCH = 1536
PATCHES = 8
SEQ = 12288
SECTIONS = 8


def current_patches(key):
    tick = jax.random.randint(jax.random.fold_in(key, 3), (), 0, SECTIONS - 1)
    return jnp.mod(tick - jnp.arange(SECTIONS), PATCHES).astype(jnp.int32)


def draw_query(key, part):
    key = jax.random.fold_in(key, 1)
    drawn = jax.random.normal(key, (SECTIONS, PATCH, D), jnp.float32)
    return drawn.astype(jnp.bfloat16)


def draw_stale_keys(key, part):
    key = jax.random.fold_in(key, 2)
    drawn = jax.random.normal(key, (SECTIONS, SEQ, D), jnp.float32)
    return drawn.astype(jnp.bfloat16)


def draw_patch_index(key, part):
    return current_patches(key)


def block_scale(stream_key, extent, pieces, smallest, high):
    factor_of, own = 1.0, jax.random.fold_in(stream_key, 6)
    for position, shards_of in pieces:
        draws = jnp.exp(jax.random.uniform(jax.random.fold_in(own, position), (shards_of,), jnp.float32, smallest / len(pieces), high / len(pieces)))
        factor_of = factor_of * jnp.repeat(draws, extent[position] // shards_of).reshape([-1 if axis == position else 1 for axis in range(len(extent))])
    return factor_of


def noise(rng, shape, spread, reach, cuts=(), kind=jnp.bfloat16):
    values = jax.random.normal(rng, shape, jnp.float32) * spread
    if len(cuts) > 0:
        values = block_scale(rng, shape, cuts, -0.22, 0.18) * values
    return jnp.clip(values, min=-reach, max=reach).astype(kind)


def setup_inputs(seed: int = 0) -> dict:
    key_list = jax.random.split(jax.random.key(seed), 8)
    query = draw_query(jax.random.fold_in(key_list[7], 71), 0)
    fresh_keys = noise(key_list[1], (SECTIONS, PATCH, D), 1.0, 6.0, ((0, 8), (1, 32)))
    fresh_values = noise(key_list[2], (SECTIONS, PATCH, D), 1.0, 6.0, ((0, 8), (1, 32)))
    stale_keys = draw_stale_keys(jax.random.fold_in(key_list[7], 71), 0)
    stale_values = noise(key_list[4], (SECTIONS, SEQ, D), 1.0, 6.0, ((0, 8), (2, 32)))
    next_gain = jnp.clip(1.0 + 0.18 * jax.random.normal(key_list[5], (SECTIONS, D), jnp.float32), 0.1, 1.9)
    patch_index = draw_patch_index(jax.random.fold_in(key_list[7], 71), 0)
    return {"query": query, "fresh_keys": fresh_keys, "fresh_values": fresh_values, "stale_keys": stale_keys, "stale_values": stale_values, "next_gain": next_gain, "patch_index": patch_index}


def head_attention(inputs):
    query_head, key_head, value_head = inputs
    scores = lax.dot_general(query_head, key_head, (((1,), (1,)), ((), ())), preferred_element_type=jnp.float32) * HD ** (-0.5)
    highest = lax.optimization_barrier(jnp.max(scores, axis=1, keepdims=True))
    weights = jnp.exp(scores - highest)
    weighted = jnp.dot(weights.astype(jnp.bfloat16), value_head, preferred_element_type=jnp.float32)
    return (weighted / lax.optimization_barrier(jnp.sum(weights, axis=1, keepdims=True))).astype(jnp.bfloat16)

def split_heads(matrix):
    return matrix.reshape(matrix.shape[0], HEADS, HD).transpose(1, 0, 2)

def section_attention(inputs):
    query_rows, fresh_k, fresh_v, cache_k, cache_v, patch_number = inputs
    first_row = (patch_number * PATCH).astype(jnp.int32)
    zero_index = jnp.zeros((), jnp.int32)
    key_rows = lax.dynamic_update_slice(cache_k, fresh_k, (first_row, zero_index))
    value_rows = lax.dynamic_update_slice(cache_v, fresh_v, (first_row, zero_index))
    heads = lax.map(head_attention, (split_heads(query_rows), split_heads(key_rows), split_heads(value_rows)))
    return heads.transpose(1, 0, 2).reshape(PATCH, D)

def reference(query, fresh_keys, fresh_values, stale_keys, stale_values, next_gain, patch_index):
    attended = lax.map(section_attention, (query, fresh_keys, fresh_values, stale_keys, stale_values, patch_index))
    arriving = jnp.roll(attended, 1, axis=0).astype(jnp.float32)
    mean_square = lax.optimization_barrier(jnp.mean(arriving * arriving, axis=2, keepdims=True))
    normed = arriving * lax.rsqrt(mean_square + 1e-06) * next_gain[:, None, :]
    return normed.astype(jnp.bfloat16)
```

```python
import functools
import math

import jax
import jax.numpy as jnp
from jax import lax
from jax.experimental import pallas as pl
from jax.experimental.pallas import tpu as pltpu
from jax.sharding import PartitionSpec as P

MESH = pl.DeviceIdType.MESH
NT = (((1,), (1,)), ((), ()))
SIDE = 4

FIRST = ((0, 0), (0, 1), (0, 3), (1, 0))
MIDDLE = ((3, 0), (0, 2), (2, 0), (1, 2), (3, 2), (2, 1), (2, 3), (2, 2))
LAST = ((1, 1), (3, 3), (1, 3), (3, 1))
GROUPS = tuple(
    tuple((dx, dy, dc) for dx, dy in chips for dc in (0, 1)) for chips in (FIRST, MIDDLE, LAST)
)
SLOTS = sum(GROUPS, ())


def lane_max(scores):
    width = 128
    highest = scores[:, :width]
    for start in range(width, scores.shape[1], width):
        highest = jnp.maximum(highest, scores[:, start : start + width])
    return jnp.max(highest, axis=1, keepdims=True)


def kernel(
    scale,
    patch_ref,
    query_ref,
    fresh_k_ref,
    fresh_v_ref,
    stale_k_ref,
    stale_v_ref,
    gain_ref,
    out_ref,
    keys,
    values,
    q_all,
    new_k,
    new_v,
    done,
    arrived,
    s0,
    s1,
    m0,
    m1,
    weighted,
    total,
    running,
    load_sem,
    q_sem,
    kv_sem,
    send_sem,
    out_send_sem,
    out_recv_sem,
    ready_sem,
):
    section = lax.axis_index("section")
    me = lax.axis_index("uly")
    sections = lax.axis_size("section")
    after = lax.rem(section + 1, sections)
    before = lax.rem(section + sections - 1, sections)
    x, y, core = me // (2 * SIDE), lax.rem(me // 2, SIDE), lax.rem(me, 2)
    rows, head = query_ref.shape[0], keys.shape[1]
    patch = q_all.shape[0]
    patches = keys.shape[0] // patch

    def device(dx, dy, dc):
        other = core if dc == 0 else 1 - core
        return (lax.rem(x + dx, SIDE) * SIDE + lax.rem(y + dy, SIDE)) * 2 + other

    def owner(slot):
        return device(*slot)

    def holder(slot):
        dx, dy, dc = slot
        return device((SIDE - dx) % SIDE, (SIDE - dy) % SIDE, dc)

    def columns(device_index):
        return pl.ds(pl.multiple_of(device_index * head, head), head)

    load_k = pltpu.make_async_copy(stale_k_ref, keys, load_sem.at[0])
    load_v = pltpu.make_async_copy(stale_v_ref, values, load_sem.at[1])
    load_k.start()
    load_v.start()

    barrier = pltpu.get_barrier_semaphore()
    for slot in SLOTS[1:]:
        pl.semaphore_signal(barrier, inc=1, device_id=(section, owner(slot)), device_id_type=MESH)
    pl.semaphore_signal(barrier, inc=1, device_id=(after, me), device_id_type=MESH)
    pl.semaphore_wait(barrier, len(SLOTS))
    pl.semaphore_signal(ready_sem, inc=1, device_id=(before, me), device_id_type=MESH)

    def send(source, k, target, send_to, receive_to):
        slot = SLOTS[k]
        if k == 0:
            pltpu.make_async_copy(
                source.at[:, columns(me)], target.at[pl.ds(0, rows), :], receive_to
            ).start()
            return
        there = holder(slot)
        pltpu.make_async_remote_copy(
            src_ref=source.at[:, columns(there)],
            dst_ref=target.at[pl.ds(k * rows, rows), :],
            send_sem=send_to,
            recv_sem=receive_to,
            device_id=(section, there),
            device_id_type=MESH,
        ).start()

    bounds, first = [], 0
    for g, group in enumerate(GROUPS):
        for k in range(first, first + len(group)):
            send(query_ref, k, q_all, send_sem.at[0], q_sem.at[g])
        bounds.append((first, first + len(group)))
        first += len(group)
    for k in range(len(SLOTS)):
        send(fresh_k_ref, k, new_k, send_sem.at[1], kv_sem.at[0])
        send(fresh_v_ref, k, new_v, send_sem.at[2], kv_sem.at[1])

    def await_bytes(ref, sem):
        pltpu.make_async_copy(ref, ref, sem).wait()

    weighted[...] = jnp.zeros_like(weighted)
    total[...] = jnp.zeros_like(total)
    scores_of, highest_of = (s0, s1), (m0, m1)
    own_patch = patch_ref[0]

    def stale_block(ref, j):
        here = ref[pl.ds(pl.multiple_of(j * patch, patch), patch), :]
        later = ref[pl.ds(pl.multiple_of((j + 1) * patch, patch), patch), :]
        return jnp.where(own_patch > j, here, later)

    def score(low, high, j, b):
        n = high - low
        block = new_k[...] if j is None else stale_block(keys, j)
        s = lax.dot_general(q_all[low:high, :], block, NT, preferred_element_type=jnp.float32)
        scores_of[b][:n, :] = s
        highest_of[b][:n, :] = jnp.broadcast_to(lane_max(s), (n, 128))

    def weigh(low, high, j, b):
        n = high - low
        old = running[:n, :]
        new = jnp.maximum(old, highest_of[b][:n, :])
        running[:n, :] = new
        faded = jnp.exp2((old - new) * scale)
        wide = jnp.concatenate([new] * (patch // 128), axis=1)
        w = jnp.exp2((scores_of[b][:n, :] - wide) * scale).astype(jnp.bfloat16)
        block = new_v[...] if j is None else stale_block(values, j)
        block = jnp.concatenate([block, jnp.ones_like(block)], axis=1)
        product = jnp.dot(w, block, preferred_element_type=jnp.float32)
        weighted[:n, :] = weighted[:n, :] * faded + product[:, :head]
        total[:n, :] = total[:n, :] * faded + product[:, head:]

    load_k.wait()
    for g, (low_slot, high_slot) in enumerate(bounds):
        low, high = low_slot * rows, high_slot * rows
        running[...] = jnp.full_like(running, -jnp.inf)
        if g == 0:
            await_bytes(q_all.at[pl.ds(low, high - low), :], q_sem.at[g])
            score(low, high, 0, 0)
            load_v.wait()

        def two_blocks(u, carry, low=low, high=high):
            score(low, high, 2 * u + 1, 1)
            weigh(low, high, 2 * u, 0)
            score(low, high, 2 * u + 2, 0)
            weigh(low, high, 2 * u + 1, 1)
            return carry

        lax.fori_loop(0, (patches - 2) // 2, two_blocks, 0)
        if g == 0:
            await_bytes(new_k, kv_sem.at[0])
            await_bytes(new_v, kv_sem.at[1])
        if g + 1 < len(bounds):
            next_low, next_high = (slot * rows for slot in bounds[g + 1])
            await_bytes(q_all.at[pl.ds(next_low, next_high - next_low), :], q_sem.at[g + 1])
        score(low, high, None, 1)
        weigh(low, high, patches - 2, 0)
        if g + 1 < len(bounds):
            score(next_low, next_high, 0, 0)
        weigh(low, high, None, 1)
        n = high - low
        done[low:high, :] = (weighted[:n, :] / total[:n, :]).astype(jnp.bfloat16)
        if g == 0:
            pl.semaphore_wait(ready_sem, 1)
        for k in range(low_slot, high_slot):
            pltpu.make_async_remote_copy(
                src_ref=done.at[pl.ds(k * rows, rows), :],
                dst_ref=arrived.at[:, columns(me)],
                send_sem=out_send_sem,
                recv_sem=out_recv_sem,
                device_id=(after, owner(SLOTS[k])),
                device_id_type=MESH,
            ).start()

    for i, ref in enumerate((q_all, new_k, new_v)):
        await_bytes(ref.at[pl.ds(rows, patch - rows), :], send_sem.at[i])
    await_bytes(arrived, out_recv_sem)
    rows_in = arrived[...].astype(jnp.float32)
    mean_square = jnp.mean(rows_in * rows_in, axis=1, keepdims=True)
    out_ref[...] = (rows_in * lax.rsqrt(mean_square + 1e-06) * gain_ref[...]).astype(jnp.bfloat16)
    await_bytes(done, out_send_sem)


def shards(query, fresh_keys, fresh_values, stale_keys, stale_values, next_gain, patch_index):
    rows, width = query.shape[1:]
    length, head = stale_keys.shape[1:]
    devices = lax.axis_size("uly")
    patch = rows * devices
    scale = head ** (-0.5) / math.log(2.0)
    tallest = max(len(group) for group in GROUPS) * rows
    hbm = pl.BlockSpec(memory_space=pl.ANY)
    vmem = pl.BlockSpec(memory_space=pltpu.VMEM)
    bf16, f32 = jnp.bfloat16, jnp.float32
    out = pl.pallas_call(
        functools.partial(kernel, scale),
        out_shape=jax.ShapeDtypeStruct((rows, width), bf16),
        in_specs=[pl.BlockSpec(memory_space=pltpu.SMEM)] + [hbm] * 5 + [vmem],
        out_specs=vmem,
        scratch_shapes=[
            pltpu.VMEM((length, head), bf16),
            pltpu.VMEM((length, head), bf16),
            pltpu.VMEM((patch, head), bf16),
            pltpu.VMEM((patch, head), bf16),
            pltpu.VMEM((patch, head), bf16),
            pltpu.VMEM((patch, head), bf16),
            pltpu.VMEM((rows, width), bf16),
            pltpu.VMEM((tallest, patch), f32),
            pltpu.VMEM((tallest, patch), f32),
            pltpu.VMEM((tallest, 128), f32),
            pltpu.VMEM((tallest, 128), f32),
            pltpu.VMEM((tallest, head), f32),
            pltpu.VMEM((tallest, head), f32),
            pltpu.VMEM((tallest, 128), f32),
            pltpu.SemaphoreType.DMA((2,)),
            pltpu.SemaphoreType.DMA((len(GROUPS),)),
            pltpu.SemaphoreType.DMA((2,)),
            pltpu.SemaphoreType.DMA((3,)),
            pltpu.SemaphoreType.DMA,
            pltpu.SemaphoreType.DMA,
            pltpu.SemaphoreType.REGULAR,
        ],
        compiler_params=pltpu.CompilerParams(
            collective_id=0, has_side_effects=True, vmem_limit_bytes=56 << 20
        ),
        cost_estimate=pl.CostEstimate(
            flops=4 * patch * length * head,
            bytes_accessed=4 * length * head + 8 * rows * width,
            transcendentals=patch * length,
        ),
    )(patch_index, query[0], fresh_keys[0], fresh_values[0], stale_keys[0], stale_values[0], next_gain)
    return out[None]


def solution(mesh):
    in_specs = (
        P("section", "uly", None),
        P("section", "uly", None),
        P("section", "uly", None),
        P("section", None, "uly"),
        P("section", None, "uly"),
        P("section", None),
        P("section"),
    )
    out_specs = P("section", "uly", None)
    return jax.shard_map(shards, mesh=mesh, in_specs=in_specs, out_specs=out_specs, check_vma=False)
```

```python
import functools
import math

import jax
import jax.numpy as jnp
from jax import lax
from jax.experimental import pallas as pl
from jax.experimental.pallas import tpu as pltpu
from jax.sharding import PartitionSpec as P

MESH = pl.DeviceIdType.MESH
NT = (((1,), (1,)), ((), ()))
SIDE = 4

FIRST = ((0, 0), (0, 1), (0, 3), (1, 0))
MIDDLE = ((3, 0), (0, 2), (2, 0), (1, 2), (3, 2), (2, 1), (2, 3), (2, 2))
LAST = ((1, 1), (3, 3), (1, 3), (3, 1))
GROUPS = tuple(
    tuple((dx, dy, dc) for dx, dy in chips for dc in (0, 1)) for chips in (FIRST, MIDDLE, LAST)
)
SLOTS = sum(GROUPS, ())


def lane_max(scores):
    width = 128
    highest = scores[:, :width]
    for start in range(width, scores.shape[1], width):
        highest = jnp.maximum(highest, scores[:, start : start + width])
    return jnp.max(highest, axis=1, keepdims=True)


def kernel(
    scale,
    patch_ref,
    query_ref,
    fresh_k_ref,
    fresh_v_ref,
    stale_k_ref,
    stale_v_ref,
    arrived,
    keys,
    values,
    q_all,
    new_k,
    new_v,
    done,
    s0,
    s1,
    m0,
    m1,
    weighted,
    total,
    running,
    load_sem,
    q_sem,
    kv_sem,
    send_sem,
    out_send_sem,
    out_recv_sem,
    ready_sem,
):
    section = lax.axis_index("section")
    me = lax.axis_index("uly")
    sections = lax.axis_size("section")
    after = lax.rem(section + 1, sections)
    before = lax.rem(section + sections - 1, sections)
    x, y, core = me // (2 * SIDE), lax.rem(me // 2, SIDE), lax.rem(me, 2)
    rows, head = query_ref.shape[0], keys.shape[1]
    patch = q_all.shape[0]
    patches = keys.shape[0] // patch

    def device(dx, dy, dc):
        other = core if dc == 0 else 1 - core
        return (lax.rem(x + dx, SIDE) * SIDE + lax.rem(y + dy, SIDE)) * 2 + other

    def owner(slot):
        return device(*slot)

    def holder(slot):
        dx, dy, dc = slot
        return device((SIDE - dx) % SIDE, (SIDE - dy) % SIDE, dc)

    def columns(device_index):
        return pl.ds(pl.multiple_of(device_index * head, head), head)

    load_k = pltpu.make_async_copy(stale_k_ref, keys, load_sem.at[0])
    load_v = pltpu.make_async_copy(stale_v_ref, values, load_sem.at[1])
    load_k.start()
    load_v.start()

    barrier = pltpu.get_barrier_semaphore()
    for slot in SLOTS[1:]:
        pl.semaphore_signal(barrier, inc=1, device_id=(section, owner(slot)), device_id_type=MESH)
    pl.semaphore_signal(barrier, inc=1, device_id=(after, me), device_id_type=MESH)
    pl.semaphore_wait(barrier, len(SLOTS))
    pl.semaphore_signal(ready_sem, inc=1, device_id=(before, me), device_id_type=MESH)

    def send(source, k, target, send_to, receive_to):
        slot = SLOTS[k]
        if k == 0:
            pltpu.make_async_copy(
                source.at[:, columns(me)], target.at[pl.ds(0, rows), :], receive_to
            ).start()
            return
        there = holder(slot)
        pltpu.make_async_remote_copy(
            src_ref=source.at[:, columns(there)],
            dst_ref=target.at[pl.ds(k * rows, rows), :],
            send_sem=send_to,
            recv_sem=receive_to,
            device_id=(section, there),
            device_id_type=MESH,
        ).start()

    bounds, first = [], 0
    for g, group in enumerate(GROUPS):
        for k in range(first, first + len(group)):
            send(query_ref, k, q_all, send_sem.at[0], q_sem.at[g])
        bounds.append((first, first + len(group)))
        first += len(group)

    def await_bytes(ref, sem):
        pltpu.make_async_copy(ref, ref, sem).wait()

    running[...] = jnp.full_like(running, -jnp.inf)
    weighted[...] = jnp.zeros_like(weighted)
    total[...] = jnp.zeros_like(total)
    scores_of, highest_of = (s0, s1), (m0, m1)
    own_patch = patch_ref[0]

    def stale_block(ref, j):
        here = ref[pl.ds(pl.multiple_of(j * patch, patch), patch), :]
        later = ref[pl.ds(pl.multiple_of((j + 1) * patch, patch), patch), :]
        return jnp.where(own_patch > j, here, later)

    def score(span, j, b):
        low, high = span
        n = high - low
        block = new_k[...] if j is None else stale_block(keys, j)
        s = lax.dot_general(q_all[low:high, :], block, NT, preferred_element_type=jnp.float32)
        scores_of[b][:n, :] = s
        highest_of[b][:n, :] = jnp.broadcast_to(lane_max(s), (n, 128))

    def weigh(span, j, b):
        low, high = span
        n = high - low
        old = running[low:high, :]
        new = jnp.maximum(old, highest_of[b][:n, :])
        running[low:high, :] = new
        faded = jnp.exp2((old - new) * scale)
        wide = jnp.concatenate([new] * (patch // 128), axis=1)
        w = jnp.exp2((scores_of[b][:n, :] - wide) * scale).astype(jnp.bfloat16)
        block = new_v[...] if j is None else stale_block(values, j)
        block = jnp.concatenate([block, jnp.ones_like(block)], axis=1)
        product = jnp.dot(w, block, preferred_element_type=jnp.float32)
        weighted[low:high, :] = weighted[low:high, :] * faded + product[:, :head]
        total[low:high, :] = total[low:high, :] * faded + product[:, head:]

    spans = [(low * rows, high * rows) for low, high in bounds]

    def await_queries(g):
        low, high = spans[g]
        await_bytes(q_all.at[pl.ds(low, high - low), :], q_sem.at[g])

    def stale_blocks(span, b):
        def two(u, carry):
            score(span, 2 * u + 1, 1 - b)
            weigh(span, 2 * u, b)
            score(span, 2 * u + 2, b)
            weigh(span, 2 * u + 1, 1 - b)
            return carry

        lax.fori_loop(0, (patches - 2) // 2, two, 0)

    def hand_on(g):
        low, high = spans[g]
        done[low:high, :] = (weighted[low:high, :] / total[low:high, :]).astype(jnp.bfloat16)
        for k in range(*bounds[g]):
            pltpu.make_async_remote_copy(
                src_ref=done.at[pl.ds(k * rows, rows), :],
                dst_ref=arrived.at[:, columns(me)],
                send_sem=out_send_sem,
                recv_sem=out_recv_sem,
                device_id=(after, owner(SLOTS[k])),
                device_id_type=MESH,
            ).start()

    near, far, late = spans
    final = patches - 2
    load_k.wait()
    await_queries(0)
    score(near, 0, 0)
    for k in range(len(SLOTS)):
        send(fresh_k_ref, k, new_k, send_sem.at[1], kv_sem.at[0])
        send(fresh_v_ref, k, new_v, send_sem.at[2], kv_sem.at[1])
    load_v.wait()
    stale_blocks(near, 0)
    await_queries(1)
    score(far, 0, 1)
    weigh(near, final, 0)
    stale_blocks(far, 1)
    await_bytes(new_k, kv_sem.at[0])
    score(near, None, 0)
    weigh(far, final, 1)
    await_bytes(new_v, kv_sem.at[1])
    score(far, None, 1)
    weigh(near, None, 0)
    pl.semaphore_wait(ready_sem, 1)
    hand_on(0)
    await_queries(2)
    score(late, 0, 0)
    weigh(far, None, 1)
    hand_on(1)
    stale_blocks(late, 0)
    score(late, None, 1)
    weigh(late, final, 0)
    weigh(late, None, 1)
    hand_on(2)

    for i, ref in enumerate((q_all, new_k, new_v)):
        await_bytes(ref.at[pl.ds(rows, patch - rows), :], send_sem.at[i])
    await_bytes(done, out_send_sem)
    await_bytes(arrived, out_recv_sem)


def norm_kernel(rows_ref, gain_ref, out_ref):
    rows = rows_ref[...].astype(jnp.float32)
    mean_square = jnp.mean(rows * rows, axis=1, keepdims=True)
    out_ref[...] = (rows * lax.rsqrt(mean_square + 1e-06) * gain_ref[...]).astype(jnp.bfloat16)


def shards(query, fresh_keys, fresh_values, stale_keys, stale_values, next_gain, patch_index):
    rows, width = query.shape[1:]
    length, head = stale_keys.shape[1:]
    devices = lax.axis_size("uly")
    patch = rows * devices
    scale = head ** (-0.5) / math.log(2.0)
    tallest = max(len(group) for group in GROUPS) * rows
    hbm = pl.BlockSpec(memory_space=pl.ANY)
    bf16, f32 = jnp.bfloat16, jnp.float32
    arriving = pl.pallas_call(
        functools.partial(kernel, scale),
        out_shape=jax.ShapeDtypeStruct((rows, width), bf16),
        in_specs=[pl.BlockSpec(memory_space=pltpu.SMEM)] + [hbm] * 5,
        out_specs=hbm,
        scratch_shapes=[
            pltpu.VMEM((length, head), bf16),
            pltpu.VMEM((length, head), bf16),
            pltpu.VMEM((patch, head), bf16),
            pltpu.VMEM((patch, head), bf16),
            pltpu.VMEM((patch, head), bf16),
            pltpu.VMEM((patch, head), bf16),
            pltpu.VMEM((tallest, patch), f32),
            pltpu.VMEM((tallest, patch), f32),
            pltpu.VMEM((tallest, 128), f32),
            pltpu.VMEM((tallest, 128), f32),
            pltpu.VMEM((patch, head), f32),
            pltpu.VMEM((patch, head), f32),
            pltpu.VMEM((patch, 128), f32),
            pltpu.SemaphoreType.DMA((2,)),
            pltpu.SemaphoreType.DMA((len(GROUPS),)),
            pltpu.SemaphoreType.DMA((2,)),
            pltpu.SemaphoreType.DMA((3,)),
            pltpu.SemaphoreType.DMA,
            pltpu.SemaphoreType.DMA,
            pltpu.SemaphoreType.REGULAR,
        ],
        compiler_params=pltpu.CompilerParams(
            collective_id=0, has_side_effects=True, vmem_limit_bytes=56 << 20
        ),
        cost_estimate=pl.CostEstimate(
            flops=4 * patch * length * head,
            bytes_accessed=4 * length * head + 8 * rows * width,
            transcendentals=patch * length,
        ),
    )(patch_index, query[0], fresh_keys[0], fresh_values[0], stale_keys[0], stale_values[0])
    handoff = pl.pallas_call(norm_kernel, out_shape=jax.ShapeDtypeStruct((rows, width), bf16))(
        arriving, next_gain
    )
    return handoff[None]


def solution(mesh):
    in_specs = (
        P("section", "uly", None),
        P("section", "uly", None),
        P("section", "uly", None),
        P("section", None, "uly"),
        P("section", None, "uly"),
        P("section", None),
        P("section"),
    )
    out_specs = P("section", "uly", None)
    return jax.shard_map(shards, mesh=mesh, in_specs=in_specs, out_specs=out_specs, check_vma=False)
```

```python
import functools
import math

import jax
import jax.numpy as jnp
from jax import lax
from jax.experimental import pallas as pl
from jax.experimental.pallas import tpu as pltpu
from jax.sharding import PartitionSpec as P

MESH = pl.DeviceIdType.MESH
NT = (((1,), (1,)), ((), ()))
SIDE = 4

FIRST = ((0, 0), (0, 1), (0, 3), (0, 2))
MIDDLE = ((1, 0), (3, 0), (2, 0), (1, 2), (3, 2), (2, 1), (2, 3), (2, 2))
LAST = ((1, 1), (3, 3), (1, 3), (3, 1))
GROUPS = tuple(
    tuple((dx, dy, dc) for dx, dy in chips for dc in (0, 1)) for chips in (FIRST, MIDDLE, LAST)
)
SLOTS = sum(GROUPS, ())


def lane_max(scores):
    width = 128
    highest = scores[:, :width]
    for start in range(width, scores.shape[1], width):
        highest = jnp.maximum(highest, scores[:, start : start + width])
    return jnp.max(highest, axis=1, keepdims=True)


def kernel(
    scale,
    patch_ref,
    query_ref,
    fresh_k_ref,
    fresh_v_ref,
    stale_k_ref,
    stale_v_ref,
    arrived,
    keys,
    values,
    q_all,
    new_k,
    new_v,
    done,
    s0,
    s1,
    m0,
    m1,
    weighted,
    total,
    running,
    load_sem,
    q_sem,
    kv_sem,
    send_sem,
    out_send_sem,
    out_recv_sem,
    row_sem,
    ready_sem,
):
    section = lax.axis_index("section")
    me = lax.axis_index("uly")
    sections = lax.axis_size("section")
    after = lax.rem(section + 1, sections)
    before = lax.rem(section + sections - 1, sections)
    x, y, core = me // (2 * SIDE), lax.rem(me // 2, SIDE), lax.rem(me, 2)
    rows, head = query_ref.shape[0], keys.shape[1]
    patch = q_all.shape[0]
    patches = keys.shape[0] // patch

    def device(dx, dy, dc):
        other = core if dc == 0 else 1 - core
        return (lax.rem(x + dx, SIDE) * SIDE + lax.rem(y + dy, SIDE)) * 2 + other

    def owner(slot):
        return device(*slot)

    def holder(slot):
        dx, dy, dc = slot
        return device((SIDE - dx) % SIDE, (SIDE - dy) % SIDE, dc)

    def columns(device_index):
        return pl.ds(pl.multiple_of(device_index * head, head), head)

    load_k = pltpu.make_async_copy(stale_k_ref, keys, load_sem.at[0])
    load_v = pltpu.make_async_copy(stale_v_ref, values, load_sem.at[1])
    load_k.start()
    load_v.start()

    barrier = pltpu.get_barrier_semaphore()
    across = [(dx, 0, 0) for dx in range(1, SIDE)]
    greeted = list(GROUPS[0][1:]) + across
    for slot in greeted:
        pl.semaphore_signal(barrier, inc=1, device_id=(section, owner(slot)), device_id_type=MESH)
    pl.semaphore_signal(barrier, inc=1, device_id=(after, me), device_id_type=MESH)
    pl.semaphore_wait(barrier, len(greeted) + 1)
    for slot in across:
        pl.semaphore_signal(row_sem, inc=1, device_id=(section, owner(slot)), device_id_type=MESH)

    def send(source, k, target, send_to, receive_to):
        slot = SLOTS[k]
        if k == 0:
            pltpu.make_async_copy(
                source.at[:, columns(me)], target.at[pl.ds(0, rows), :], receive_to
            ).start()
            return
        there = holder(slot)
        pltpu.make_async_remote_copy(
            src_ref=source.at[:, columns(there)],
            dst_ref=target.at[pl.ds(k * rows, rows), :],
            send_sem=send_to,
            recv_sem=receive_to,
            device_id=(section, there),
            device_id_type=MESH,
        ).start()

    bounds, first = [], 0
    for g, group in enumerate(GROUPS):
        if g == 1:
            pl.semaphore_wait(row_sem, len(across))
            pl.semaphore_signal(ready_sem, inc=1, device_id=(before, me), device_id_type=MESH)
        for k in range(first, first + len(group)):
            send(query_ref, k, q_all, send_sem.at[0], q_sem.at[g])
        bounds.append((first, first + len(group)))
        first += len(group)

    def await_bytes(ref, sem):
        pltpu.make_async_copy(ref, ref, sem).wait()

    running[...] = jnp.full_like(running, -jnp.inf)
    weighted[...] = jnp.zeros_like(weighted)
    total[...] = jnp.zeros_like(total)
    scores_of, highest_of = (s0, s1), (m0, m1)
    own_patch = patch_ref[0]

    def stale_block(ref, j):
        here = ref[pl.ds(pl.multiple_of(j * patch, patch), patch), :]
        later = ref[pl.ds(pl.multiple_of((j + 1) * patch, patch), patch), :]
        return jnp.where(own_patch > j, here, later)

    def score(span, j, b):
        low, high = span
        n = high - low
        block = new_k[...] if j is None else stale_block(keys, j)
        s = lax.dot_general(q_all[low:high, :], block, NT, preferred_element_type=jnp.float32)
        scores_of[b][:n, :] = s
        highest_of[b][:n, :] = jnp.broadcast_to(lane_max(s), (n, 128))

    def weigh(span, j, b):
        low, high = span
        n = high - low
        old = running[low:high, :]
        new = jnp.maximum(old, highest_of[b][:n, :])
        running[low:high, :] = new
        faded = jnp.exp2((old - new) * scale)
        wide = jnp.concatenate([new] * (patch // 128), axis=1)
        w = jnp.exp2((scores_of[b][:n, :] - wide) * scale).astype(jnp.bfloat16)
        block = new_v[...] if j is None else stale_block(values, j)
        block = jnp.concatenate([block, jnp.ones_like(block)], axis=1)
        product = jnp.dot(w, block, preferred_element_type=jnp.float32)
        weighted[low:high, :] = weighted[low:high, :] * faded + product[:, :head]
        total[low:high, :] = total[low:high, :] * faded + product[:, head:]

    spans = [(low * rows, high * rows) for low, high in bounds]

    def await_queries(g):
        low, high = spans[g]
        await_bytes(q_all.at[pl.ds(low, high - low), :], q_sem.at[g])

    def stale_blocks(span, b):
        def two(u, carry):
            score(span, 2 * u + 1, 1 - b)
            weigh(span, 2 * u, b)
            score(span, 2 * u + 2, b)
            weigh(span, 2 * u + 1, 1 - b)
            return carry

        lax.fori_loop(0, (patches - 2) // 2, two, 0)

    def hand_on(g):
        low, high = spans[g]
        done[low:high, :] = (weighted[low:high, :] / total[low:high, :]).astype(jnp.bfloat16)
        for k in range(*bounds[g]):
            pltpu.make_async_remote_copy(
                src_ref=done.at[pl.ds(k * rows, rows), :],
                dst_ref=arrived.at[:, columns(me)],
                send_sem=out_send_sem,
                recv_sem=out_recv_sem,
                device_id=(after, owner(SLOTS[k])),
                device_id_type=MESH,
            ).start()

    near, far, late = spans
    final = patches - 2
    load_k.wait()
    await_queries(0)
    score(near, 0, 0)
    for k in range(len(SLOTS)):
        send(fresh_k_ref, k, new_k, send_sem.at[1], kv_sem.at[0])
        send(fresh_v_ref, k, new_v, send_sem.at[2], kv_sem.at[1])
    load_v.wait()
    stale_blocks(near, 0)
    await_queries(1)
    score(far, 0, 1)
    weigh(near, final, 0)
    stale_blocks(far, 1)
    await_bytes(new_k, kv_sem.at[0])
    score(near, None, 0)
    weigh(far, final, 1)
    await_bytes(new_v, kv_sem.at[1])
    score(far, None, 1)
    weigh(near, None, 0)
    pl.semaphore_wait(ready_sem, 1)
    hand_on(0)
    await_queries(2)
    score(late, 0, 0)
    weigh(far, None, 1)
    hand_on(1)
    stale_blocks(late, 0)
    score(late, None, 1)
    weigh(late, final, 0)
    weigh(late, None, 1)
    hand_on(2)

    for i, ref in enumerate((q_all, new_k, new_v)):
        await_bytes(ref.at[pl.ds(rows, patch - rows), :], send_sem.at[i])
    await_bytes(done, out_send_sem)
    await_bytes(arrived, out_recv_sem)


def norm_kernel(rows_ref, gain_ref, out_ref):
    rows = rows_ref[...].astype(jnp.float32)
    mean_square = jnp.mean(rows * rows, axis=1, keepdims=True)
    out_ref[...] = (rows * lax.rsqrt(mean_square + 1e-06) * gain_ref[...]).astype(jnp.bfloat16)


def shards(query, fresh_keys, fresh_values, stale_keys, stale_values, next_gain, patch_index):
    rows, width = query.shape[1:]
    length, head = stale_keys.shape[1:]
    devices = lax.axis_size("uly")
    patch = rows * devices
    scale = head ** (-0.5) / math.log(2.0)
    tallest = max(len(group) for group in GROUPS) * rows
    hbm = pl.BlockSpec(memory_space=pl.ANY)
    bf16, f32 = jnp.bfloat16, jnp.float32
    arriving = pl.pallas_call(
        functools.partial(kernel, scale),
        out_shape=jax.ShapeDtypeStruct((rows, width), bf16),
        in_specs=[pl.BlockSpec(memory_space=pltpu.SMEM)] + [hbm] * 5,
        out_specs=hbm,
        scratch_shapes=[
            pltpu.VMEM((length, head), bf16),
            pltpu.VMEM((length, head), bf16),
            pltpu.VMEM((patch, head), bf16),
            pltpu.VMEM((patch, head), bf16),
            pltpu.VMEM((patch, head), bf16),
            pltpu.VMEM((patch, head), bf16),
            pltpu.VMEM((tallest, patch), f32),
            pltpu.VMEM((tallest, patch), f32),
            pltpu.VMEM((tallest, 128), f32),
            pltpu.VMEM((tallest, 128), f32),
            pltpu.VMEM((patch, head), f32),
            pltpu.VMEM((patch, head), f32),
            pltpu.VMEM((patch, 128), f32),
            pltpu.SemaphoreType.DMA((2,)),
            pltpu.SemaphoreType.DMA((len(GROUPS),)),
            pltpu.SemaphoreType.DMA((2,)),
            pltpu.SemaphoreType.DMA((3,)),
            pltpu.SemaphoreType.DMA,
            pltpu.SemaphoreType.DMA,
            pltpu.SemaphoreType.REGULAR,
            pltpu.SemaphoreType.REGULAR,
        ],
        compiler_params=pltpu.CompilerParams(
            collective_id=0, has_side_effects=True, vmem_limit_bytes=56 << 20
        ),
        cost_estimate=pl.CostEstimate(
            flops=4 * patch * length * head,
            bytes_accessed=4 * length * head + 8 * rows * width,
            transcendentals=patch * length,
        ),
    )(patch_index, query[0], fresh_keys[0], fresh_values[0], stale_keys[0], stale_values[0])
    handoff = pl.pallas_call(norm_kernel, out_shape=jax.ShapeDtypeStruct((rows, width), bf16))(
        arriving, next_gain
    )
    return handoff[None]


def solution(mesh):
    in_specs = (
        P("section", "uly", None),
        P("section", "uly", None),
        P("section", "uly", None),
        P("section", None, "uly"),
        P("section", None, "uly"),
        P("section", None),
        P("section"),
    )
    out_specs = P("section", "uly", None)
    return jax.shard_map(shards, mesh=mesh, in_specs=in_specs, out_specs=out_specs, check_vma=False)
```

```python
import functools
import math

import jax
import jax.numpy as jnp
from jax import lax
from jax.experimental import pallas as pl
from jax.experimental.pallas import tpu as pltpu
from jax.sharding import PartitionSpec as P

MESH = pl.DeviceIdType.MESH
NT = (((1,), (1,)), ((), ()))
SIDE = 4

FIRST = ((0, 0), (0, 1), (0, 3), (0, 2))
MIDDLE = ((1, 0), (3, 0), (2, 0), (1, 2), (3, 2), (2, 1), (2, 3), (2, 2))
LAST = ((1, 1), (3, 3), (1, 3), (3, 1))
GROUPS = tuple(
    tuple((dx, dy, dc) for dx, dy in chips for dc in (0, 1)) for chips in (FIRST, MIDDLE, LAST)
)
SLOTS = sum(GROUPS, ())


def lane_max(scores):
    width = 128
    highest = scores[:, :width]
    for start in range(width, scores.shape[1], width):
        highest = jnp.maximum(highest, scores[:, start : start + width])
    return highest


def kernel(
    scale,
    patch_ref,
    query_ref,
    fresh_k_ref,
    fresh_v_ref,
    stale_k_ref,
    stale_v_ref,
    arrived,
    keys,
    values,
    q_all,
    new_k,
    new_v,
    done,
    s0,
    s1,
    m0,
    m1,
    weighted,
    total,
    running,
    load_sem,
    q_sem,
    kv_sem,
    send_sem,
    out_send_sem,
    out_recv_sem,
    row_sem,
    ready_sem,
):
    section = lax.axis_index("section")
    me = lax.axis_index("uly")
    sections = lax.axis_size("section")
    after = lax.rem(section + 1, sections)
    before = lax.rem(section + sections - 1, sections)
    x, y, core = me // (2 * SIDE), lax.rem(me // 2, SIDE), lax.rem(me, 2)
    rows, head = query_ref.shape[0], keys.shape[1]
    patch = q_all.shape[0]
    patches = keys.shape[0] // patch

    def device(dx, dy, dc):
        other = core if dc == 0 else 1 - core
        return (lax.rem(x + dx, SIDE) * SIDE + lax.rem(y + dy, SIDE)) * 2 + other

    def owner(slot):
        return device(*slot)

    def holder(slot):
        dx, dy, dc = slot
        return device((SIDE - dx) % SIDE, (SIDE - dy) % SIDE, dc)

    def columns(device_index):
        return pl.ds(pl.multiple_of(device_index * head, head), head)

    load_k = pltpu.make_async_copy(stale_k_ref, keys, load_sem.at[0])
    load_v = pltpu.make_async_copy(stale_v_ref, values, load_sem.at[1])
    load_k.start()
    load_v.start()

    barrier = pltpu.get_barrier_semaphore()
    across = [(dx, 0, 0) for dx in range(1, SIDE)]
    greeted = list(GROUPS[0][1:]) + across
    for slot in greeted:
        pl.semaphore_signal(barrier, inc=1, device_id=(section, owner(slot)), device_id_type=MESH)
    pl.semaphore_signal(barrier, inc=1, device_id=(after, me), device_id_type=MESH)
    pl.semaphore_wait(barrier, len(greeted) + 1)
    for slot in across:
        pl.semaphore_signal(row_sem, inc=1, device_id=(section, owner(slot)), device_id_type=MESH)

    def send(source, k, target, send_to, receive_to):
        slot = SLOTS[k]
        if k == 0:
            pltpu.make_async_copy(
                source.at[:, columns(me)], target.at[pl.ds(0, rows), :], receive_to
            ).start()
            return
        there = holder(slot)
        pltpu.make_async_remote_copy(
            src_ref=source.at[:, columns(there)],
            dst_ref=target.at[pl.ds(k * rows, rows), :],
            send_sem=send_to,
            recv_sem=receive_to,
            device_id=(section, there),
            device_id_type=MESH,
        ).start()

    bounds, first = [], 0
    for g, group in enumerate(GROUPS):
        if g == 1:
            pl.semaphore_wait(row_sem, len(across))
            pl.semaphore_signal(ready_sem, inc=1, device_id=(before, me), device_id_type=MESH)
        for k in range(first, first + len(group)):
            send(query_ref, k, q_all, send_sem.at[0], q_sem.at[g])
        bounds.append((first, first + len(group)))
        first += len(group)

    def await_bytes(ref, sem):
        pltpu.make_async_copy(ref, ref, sem).wait()

    running[...] = jnp.full_like(running, -jnp.inf)
    weighted[...] = jnp.zeros_like(weighted)
    total[...] = jnp.zeros_like(total)
    scores_of, highest_of = (s0, s1), (m0, m1)
    own_patch = patch_ref[0]

    def stale_block(ref, j):
        here = ref[pl.ds(pl.multiple_of(j * patch, patch), patch), :]
        later = ref[pl.ds(pl.multiple_of((j + 1) * patch, patch), patch), :]
        return jnp.where(own_patch > j, here, later)

    def score(span, j, b):
        low, high = span
        n = high - low
        block = new_k[...] if j is None else stale_block(keys, j)
        s = lax.dot_general(q_all[low:high, :], block, NT, preferred_element_type=jnp.float32)
        scores_of[b][:n, :] = s
        highest_of[b][:n, :] = lane_max(s)

    def weigh(span, j, b, skip=0):
        low, high = span
        stop = skip + high - low
        old = running[low:high, :]
        new = jnp.maximum(old, jnp.max(highest_of[b][skip:stop, :], axis=1, keepdims=True))
        running[low:high, :] = new
        faded = jnp.exp2((old - new) * scale)
        wide = jnp.concatenate([new] * (patch // 128), axis=1)
        w = jnp.exp2((scores_of[b][skip:stop, :] - wide) * scale).astype(jnp.bfloat16)
        block = new_v[...] if j is None else stale_block(values, j)
        block = jnp.concatenate([block, jnp.ones_like(block)], axis=1)
        product = jnp.dot(w, block, preferred_element_type=jnp.float32)
        weighted[low:high, :] = weighted[low:high, :] * faded + product[:, :head]
        total[low:high, :] = total[low:high, :] * faded + product[:, head:]

    spans = [(low * rows, high * rows) for low, high in bounds]

    def await_queries(g):
        low, high = spans[g]
        await_bytes(q_all.at[pl.ds(low, high - low), :], q_sem.at[g])

    def stale_blocks(span, b):
        def two(u, carry):
            score(span, 2 * u + 1, 1 - b)
            weigh(span, 2 * u, b)
            score(span, 2 * u + 2, b)
            weigh(span, 2 * u + 1, 1 - b)
            return carry

        lax.fori_loop(0, (patches - 2) // 2, two, 0)

    def hand_on(slots):
        low, high = slots[0] * rows, slots[1] * rows
        done[low:high, :] = (weighted[low:high, :] / total[low:high, :]).astype(jnp.bfloat16)
        for k in range(*slots):
            pltpu.make_async_remote_copy(
                src_ref=done.at[pl.ds(k * rows, rows), :],
                dst_ref=arrived.at[:, columns(me)],
                send_sem=out_send_sem,
                recv_sem=out_recv_sem,
                device_id=(after, owner(SLOTS[k])),
                device_id_type=MESH,
            ).start()

    near, far, late = spans
    final = patches - 2
    load_k.wait()
    await_queries(0)
    score(near, 0, 0)
    for k in range(len(SLOTS)):
        send(fresh_k_ref, k, new_k, send_sem.at[1], kv_sem.at[0])
        send(fresh_v_ref, k, new_v, send_sem.at[2], kv_sem.at[1])
    load_v.wait()
    stale_blocks(near, 0)
    await_queries(1)
    score(far, 0, 1)
    weigh(near, final, 0)
    stale_blocks(far, 1)
    await_bytes(new_k, kv_sem.at[0])
    score(near, None, 0)
    weigh(far, final, 1)
    await_bytes(new_v, kv_sem.at[1])
    score(far, None, 1)
    weigh(near, None, 0)
    pl.semaphore_wait(ready_sem, 1)
    hand_on(bounds[0])
    await_queries(2)
    score(late, 0, 0)
    weigh(far, None, 1)
    hand_on(bounds[1])
    stale_blocks(late, 0)
    score(late, None, 1)
    weigh(late, final, 0)
    first, stop = bounds[2]
    middle = (first + stop) // 2
    for part in ((first, middle), (middle, stop)):
        weigh((part[0] * rows, part[1] * rows), None, 1, (part[0] - first) * rows)
        hand_on(part)

    for i, ref in enumerate((q_all, new_k, new_v)):
        await_bytes(ref.at[pl.ds(rows, patch - rows), :], send_sem.at[i])
    await_bytes(done, out_send_sem)
    await_bytes(arrived, out_recv_sem)


def norm_kernel(rows_ref, gain_ref, out_ref):
    rows = rows_ref[...].astype(jnp.float32)
    mean_square = jnp.mean(rows * rows, axis=1, keepdims=True)
    out_ref[...] = (rows * lax.rsqrt(mean_square + 1e-06) * gain_ref[...]).astype(jnp.bfloat16)


def shards(query, fresh_keys, fresh_values, stale_keys, stale_values, next_gain, patch_index):
    rows, width = query.shape[1:]
    length, head = stale_keys.shape[1:]
    devices = lax.axis_size("uly")
    patch = rows * devices
    scale = head ** (-0.5) / math.log(2.0)
    tallest = max(len(group) for group in GROUPS) * rows
    hbm = pl.BlockSpec(memory_space=pl.ANY)
    bf16, f32 = jnp.bfloat16, jnp.float32
    arriving = pl.pallas_call(
        functools.partial(kernel, scale),
        out_shape=jax.ShapeDtypeStruct((rows, width), bf16),
        in_specs=[pl.BlockSpec(memory_space=pltpu.SMEM)] + [hbm] * 5,
        out_specs=hbm,
        scratch_shapes=[
            pltpu.VMEM((length, head), bf16),
            pltpu.VMEM((length, head), bf16),
            pltpu.VMEM((patch, head), bf16),
            pltpu.VMEM((patch, head), bf16),
            pltpu.VMEM((patch, head), bf16),
            pltpu.VMEM((patch, head), bf16),
            pltpu.VMEM((tallest, patch), f32),
            pltpu.VMEM((tallest, patch), f32),
            pltpu.VMEM((tallest, 128), f32),
            pltpu.VMEM((tallest, 128), f32),
            pltpu.VMEM((patch, head), f32),
            pltpu.VMEM((patch, head), f32),
            pltpu.VMEM((patch, 128), f32),
            pltpu.SemaphoreType.DMA((2,)),
            pltpu.SemaphoreType.DMA((len(GROUPS),)),
            pltpu.SemaphoreType.DMA((2,)),
            pltpu.SemaphoreType.DMA((3,)),
            pltpu.SemaphoreType.DMA,
            pltpu.SemaphoreType.DMA,
            pltpu.SemaphoreType.REGULAR,
            pltpu.SemaphoreType.REGULAR,
        ],
        compiler_params=pltpu.CompilerParams(
            collective_id=0, has_side_effects=True, vmem_limit_bytes=56 << 20
        ),
        cost_estimate=pl.CostEstimate(
            flops=4 * patch * length * head,
            bytes_accessed=4 * length * head + 8 * rows * width,
            transcendentals=patch * length,
        ),
    )(patch_index, query[0], fresh_keys[0], fresh_values[0], stale_keys[0], stale_values[0])
    handoff = pl.pallas_call(norm_kernel, out_shape=jax.ShapeDtypeStruct((rows, width), bf16))(
        arriving, next_gain
    )
    return handoff[None]


def solution(mesh):
    in_specs = (
        P("section", "uly", None),
        P("section", "uly", None),
        P("section", "uly", None),
        P("section", None, "uly"),
        P("section", None, "uly"),
        P("section", None),
        P("section"),
    )
    out_specs = P("section", "uly", None)
    return jax.shard_map(shards, mesh=mesh, in_specs=in_specs, out_specs=out_specs, check_vma=False)
```
